32 devices in a mesh: groups: 2 (over y), mpo: 4 (over z), sector: 4 (over x, core).
Axes of the slice: x: 2, y: 2, z: 4, core: 2. Of those that a mesh axis runs over, the one named last changes fastest.
Arguments:
- psi: bfloat16 [16, 128, 16, 128], P(('groups', 'sector')), parts along dimension 0, may hold values from -6 to 6
- left_env: bfloat16 [4, 128, 128, 128], P('mpo', ('groups', 'sector')), parts along dimension 1, may hold values from -0.5 to 0.5
- mpo: bfloat16 [8, 4, 16, 16], P(('groups', 'mpo')), parts along dimension 0, may hold values from -0.75 to 0.75
- right_env: bfloat16 [4, 128, 128, 128], P('mpo', ('groups', 'sector')), parts along dimension 1, may hold values from -0.25 to 0.25
- left_local: int32 [16], P('groups'), parts along dimension 0, may hold values from 0 to 15
- right_owner: int32 [16], P('groups'), parts along dimension 0, may hold values from 0 to 3, as said below
- right_local: int32 [16], P('groups'), parts along dimension 0, may hold values from 0 to 15
Outputs:
- h_psi: bfloat16 [16, 262144], P(('groups', 'sector'), 'mpo'), parts along dimension 0
The draws below stay inside these ranges and needn't reach their ends.
There are 2 independent parts, one for each index of `groups`. The reference program is written for one: setup_inputs(seed, part) draws one part's arguments, and reference() takes and returns one part's arrays. A program takes and returns all parts, laid end to end along the dimension named above; each array names one. Nothing has to cross between parts.
Inputs may be any that keep to these rules, and one draw needn't show every extreme that they name: `right_owner`: two indices of sector have all their blocks' right sectors owned by one common index, which owns exactly 4 blocks' right sectors; no block of any other index goes to that owner, and no index owns more than 4.
All inputs are finite; a program needn't handle non-finite values.
Results may differ from the reference program's by a relative error of at most 0.0058.
Values may be sent and summed in bfloat16 or wider, within the bound.
A program may use at most 128 MiB of HBM per device.

```python
import jax
import jax.numpy as jnp
from jax import lax

B = 128
PHYS = 16
SEC_DEV = 16
BLK_DEV = 2
MPO_BOND = 4
NSEC = 64
NBLK = 8
N_SECTOR = 4


def draw_right_owner(key, part):
    key = jax.random.fold_in(key, 7)
    key_hot, key_src, key_rest = jax.random.split(key, 3)
    hot = jax.random.randint(key_hot, (), 0, N_SECTOR)
    order = jax.random.permutation(key_src, N_SECTOR)
    chosen = order[:, None] < 2
    others = jax.random.randint(key_rest, (N_SECTOR, BLK_DEV), 0, N_SECTOR - 1)
    others = others + (others >= hot).astype(jnp.int32)
    owner = jnp.where(chosen, hot, others)
    return owner.reshape(NBLK).astype(jnp.int32)


def with_ends(entries, own_key, least, largest):
    spot = [jax.random.randint(jax.random.fold_in(own_key, axis), (), 0, length) for axis, length in enumerate(entries.shape)]
    widest = entries.shape.index(max(entries.shape))
    beside = spot[:widest] + [(spot[widest] + 1) % entries.shape[widest]] + spot[widest + 1:]
    return entries.at[tuple(spot)].set(least).at[tuple(beside)].set(largest)


def levels(own_key, shape, cuts, low, top_value):
    gain, own = 1.0, jax.random.fold_in(own_key, 6)
    for position, blocks in cuts:
        draws = jnp.exp(jax.random.uniform(jax.random.fold_in(own, position), (blocks,), jnp.float32, low / len(cuts), top_value / len(cuts)))
        gain = gain * jnp.repeat(draws, shape[position] // blocks).reshape([-1 if axis == position else 1 for axis in range(len(shape))])
    return gain


def gaussian(stream_key, dims, scale, most, cuts=(), dtype=jnp.bfloat16):
    values = scale * jax.random.normal(stream_key, dims, jnp.float32)
    if cuts:
        values = values * levels(stream_key, dims, cuts, -0.22, 0.18)
    return jnp.clip(values, -most, most).astype(dtype)


def setup_inputs(seed: int = 0, part: int = 0) -> dict:
    splits = jax.random.split(jax.random.key(seed), 8)
    own_keys = jax.random.split(jax.random.fold_in(splits[7], part), 8)
    psi = gaussian(own_keys[0], (NBLK, B, PHYS, B), 1.0, 6.0, ((0, 4),))
    left_env = gaussian(own_keys[1], (MPO_BOND, NSEC, B, B), B ** -0.5, 0.5, ((0, 4), (1, 4)))
    mpo = gaussian(own_keys[2], (MPO_BOND, MPO_BOND, PHYS, PHYS), (PHYS * MPO_BOND) ** -0.5, 0.75, ((0, 4),))
    right_env = gaussian(own_keys[3], (MPO_BOND, NSEC, B, B), (B * MPO_BOND) ** -0.5, 0.25, ((0, 4), (1, 4)))
    left_local = with_ends(jax.random.randint(own_keys[4], (NBLK,), 0, SEC_DEV), jax.random.fold_in(own_keys[4], 1), 0, SEC_DEV - 1).astype(jnp.int32)
    right_owner = draw_right_owner(jax.random.fold_in(jax.random.fold_in(splits[7], part), 71), part)
    right_local = with_ends(jax.random.randint(own_keys[6], (NBLK,), 0, SEC_DEV), jax.random.fold_in(own_keys[6], 1), 0, SEC_DEV - 1).astype(jnp.int32)
    return {"psi": psi, "left_env": left_env, "mpo": mpo, "right_env": right_env, "left_local": left_local, "right_owner": right_owner, "right_local": right_local}


def reference(psi, left_env, mpo, right_env, left_local, right_owner, right_local):
    owners = (jnp.arange(NBLK) // BLK_DEV).astype(jnp.int32)
    left_sector = (owners * SEC_DEV + left_local).astype(jnp.int32)
    right_sector = (right_owner * SEC_DEV + right_local).astype(jnp.int32)

    def one_block(index):
        block = psi[index].reshape(B, PHYS * B)
        lenv = left_env[:, left_sector[index]]
        renv = right_env[:, right_sector[index]]
        stacked = jnp.transpose(renv, (0, 2, 1)).reshape(MPO_BOND * B, B)

        def per_index(total, w):
            moved = jnp.dot(lenv[w], block, preferred_element_type=jnp.float32).astype(jnp.bfloat16)
            moved = moved.reshape(B, PHYS, B)
            mixed = jnp.einsum('vqp,lpr->lqvr', mpo[w].astype(jnp.float32), moved.astype(jnp.float32))
            mixed = mixed.astype(jnp.bfloat16).reshape(B * PHYS, MPO_BOND * B)
            return total + jnp.dot(mixed, stacked, preferred_element_type=jnp.float32), None

        total, unused = lax.scan(per_index, jnp.zeros((B * PHYS, B), jnp.float32), jnp.arange(MPO_BOND))
        return total.astype(jnp.bfloat16).reshape(B * PHYS * B)

    return lax.map(one_block, jnp.arange(NBLK))
```

```python
import jax
import jax.numpy as jnp
from jax import lax
from jax.sharding import PartitionSpec as P

F32 = jnp.float32
BF16 = jnp.bfloat16


def body(psi, left_env, mpo, right_env, left_local, right_owner, right_local):
    blk_dev, rows, phys, width = psi.shape
    nsec = lax.axis_size("sector")
    nmpo = lax.axis_size("mpo")
    local_rows = rows // nmpo
    me = lax.axis_index("sector")
    first = me * blk_dev
    slots = jnp.where(right_owner == me, right_local, 0)
    wanted = [lax.dynamic_index_in_dim(right_env[0], slots[i], 0) for i in range(nsec * blk_dev)]
    outgoing = jnp.concatenate(wanted).reshape(nsec, blk_dev, rows, width)
    arrived = lax.all_to_all(outgoing, "sector", split_axis=0, concat_axis=0, tiled=True)

    own_left, own_env = [], []
    for i in range(blk_dev):
        own_left.append(
            lax.dynamic_index_in_dim(left_env[0], left_local[first + i], 0).reshape(nmpo, local_rows, rows)
        )
        own_env.append(lax.dynamic_index_in_dim(arrived[:, i], right_owner[first + i], 0))
    env_rows = blk_dev * rows
    own_env = jnp.concatenate(own_env).reshape(1, env_rows, width)
    left_rows = blk_dev * local_rows
    own_mpo = mpo[0].reshape(1, -1, width)
    packed = jnp.concatenate(
        own_left
        + [
            jnp.broadcast_to(own_env, (nmpo, env_rows, width)),
            jnp.broadcast_to(own_mpo, (nmpo,) + own_mpo.shape[1:]),
        ],
        axis=1,
    )
    got = lax.all_to_all(packed, "mpo", split_axis=0, concat_axis=0, tiled=True)
    lenv = got[:, :left_rows].reshape(nmpo, blk_dev, local_rows, rows)
    renv = got[:, left_rows : left_rows + env_rows].reshape(nmpo, blk_dev, rows, width)
    tensor = got[:, left_rows + env_rows :].reshape((nmpo,) + mpo.shape[1:])

    moved = jnp.einsum("wkml,klpr->kmwpr", lenv, psi, preferred_element_type=F32).astype(BF16)
    mixed = jnp.einsum("wvqp,kmwpr->kmqvr", tensor, moved, preferred_element_type=F32).astype(BF16)
    result = jnp.einsum("kmqvr,vktr->kmqt", mixed, renv, preferred_element_type=F32).astype(BF16)
    return result.reshape(blk_dev, local_rows * phys * width)


def solution(mesh):
    placed = (
        P(("groups", "sector"), None, None, None),
        P("mpo", ("groups", "sector"), None, None),
        P(("groups", "mpo"), None, None, None),
        P("mpo", ("groups", "sector"), None, None),
        P("groups"),
        P("groups"),
        P("groups"),
    )
    return jax.shard_map(
        body, mesh=mesh, in_specs=placed, out_specs=P(("groups", "sector"), "mpo"), check_vma=False
    )
```

```python
import functools

import jax
import jax.numpy as jnp
from jax import lax
from jax.experimental import pallas as pl
from jax.experimental.pallas import tpu as pltpu
from jax.sharding import PartitionSpec as P

F32 = jnp.float32
BF16 = jnp.bfloat16
MESH = pl.DeviceIdType.MESH


def exchange(
    nsec,
    nmpo,
    left_local,
    right_owner,
    right_local,
    left_env,
    right_env,
    mpo,
    lenv,
    renv,
    tensor,
    to_sector,
    to_mpo,
    sector_send,
    sector_recv,
    left_send,
    left_recv,
    tensor_send,
    tensor_recv,
    up_send,
    down_send,
    line_recv,
    *from_sector,
):
    blk_dev, local_rows = lenv.shape[1], lenv.shape[2]
    me = lax.axis_index("sector")
    z = lax.axis_index("mpo")
    barrier = pltpu.get_barrier_semaphore()
    for d in range(1, nsec):
        pl.semaphore_signal(barrier, inc=1, device_id={"sector": lax.rem(me + d, nsec)}, device_id_type=MESH)
    for d in range(1, nmpo):
        pl.semaphore_signal(barrier, inc=1, device_id={"mpo": lax.rem(z + d, nmpo)}, device_id_type=MESH)

    for k in range(blk_dev):
        for t in range(nsec):
            to_sector[k, t] = right_env[right_local[t * blk_dev + k]]
    for k in range(blk_dev):
        picked = left_env[left_local[me * blk_dev + k]]
        for j in range(nmpo):
            to_mpo[j, k] = picked[j * local_rows : (j + 1) * local_rows]

    pl.semaphore_wait(barrier, nsec + nmpo - 2)

    def sector_copy(k, d):
        peer = lax.rem(me + d, nsec)
        return pltpu.make_async_remote_copy(
            src_ref=to_sector.at[k, peer],
            dst_ref=from_sector[k].at[me],
            send_sem=sector_send.at[k, d],
            recv_sem=sector_recv.at[k, d],
            device_id={"sector": peer},
            device_id_type=MESH,
        )

    def left_copy(d):
        peer = lax.rem(z + d, nmpo)
        return pltpu.make_async_remote_copy(
            src_ref=to_mpo.at[peer],
            dst_ref=lenv.at[z],
            send_sem=left_send.at[d],
            recv_sem=left_recv.at[d],
            device_id={"mpo": peer},
            device_id_type=MESH,
        )

    def tensor_copy(d):
        return pltpu.make_async_remote_copy(
            src_ref=mpo.at[0],
            dst_ref=tensor.at[z],
            send_sem=tensor_send.at[d],
            recv_sem=tensor_recv.at[d],
            device_id={"mpo": lax.rem(z + d, nmpo)},
            device_id_type=MESH,
        )

    def line_copy(origin, k, up):
        sems = up_send if up else down_send
        return pltpu.make_async_remote_copy(
            src_ref=renv.at[origin, k],
            dst_ref=renv.at[origin, k],
            send_sem=sems.at[origin, k],
            recv_sem=line_recv.at[origin, k],
            device_id={"mpo": z + 1 if up else z - 1},
            device_id_type=MESH,
        )

    for k in range(blk_dev):
        for d in range(1, nsec):
            sector_copy(k, d).start()
    for d in range(1, nmpo):
        left_copy(d).start()
        tensor_copy(d).start()
    lenv[z] = to_mpo[z]
    tensor[z] = mpo[0]

    for k in range(blk_dev):
        from_sector[k][me] = to_sector[k, me]
        for d in range(1, nsec):
            sector_copy(k, d).wait_recv()
        renv[z, k] = from_sector[k][right_owner[me * blk_dev + k]]

        @pl.when(z < nmpo - 1)
        def _():
            line_copy(z, k, True).start()

        @pl.when(z > 0)
        def _():
            line_copy(z, k, False).start()

    for d in range(1, nmpo):
        for k in range(blk_dev):

            @pl.when(z - d >= 0)
            def _():
                line_copy(z - d, k, True).wait_recv()

                @pl.when(z < nmpo - 1)
                def _():
                    line_copy(z - d, k, True).start()

            @pl.when(z + d < nmpo)
            def _():
                line_copy(z + d, k, False).wait_recv()

                @pl.when(z > 0)
                def _():
                    line_copy(z + d, k, False).start()

    for d in range(1, nmpo):
        left_copy(d).wait()
        tensor_copy(d).wait()
    for k in range(blk_dev):
        for d in range(1, nsec):
            sector_copy(k, d).wait_send()
        for d in range(nmpo):

            @pl.when((z < nmpo - 1) & (z - d >= 0))
            def _():
                line_copy(z - d, k, True).wait_send()

            @pl.when((z > 0) & (z + d < nmpo))
            def _():
                line_copy(z + d, k, False).wait_send()


def gather(nsec, nmpo, mpo, left_env, right_env, left_local, right_owner, right_local, blk_dev):
    rows, width = right_env.shape[2:]
    local_rows = rows // nmpo
    vmem = pl.BlockSpec(memory_space=pltpu.VMEM)
    smem = pl.BlockSpec(memory_space=pltpu.SMEM)
    dma = pltpu.SemaphoreType.DMA
    return pl.pallas_call(
        functools.partial(exchange, nsec, nmpo),
        out_shape=(
            jax.ShapeDtypeStruct((nmpo, blk_dev, local_rows, rows), BF16),
            jax.ShapeDtypeStruct((nmpo, blk_dev, rows, width), BF16),
            jax.ShapeDtypeStruct((nmpo,) + mpo.shape[1:], BF16),
        ),
        in_specs=[smem] * 3 + [vmem] * 3,
        out_specs=(vmem,) * 3,
        scratch_shapes=[
            pltpu.VMEM((blk_dev, nsec, rows, width), BF16),
            pltpu.VMEM((nmpo, blk_dev, local_rows, rows), BF16),
            dma((blk_dev, nsec)),
            dma((blk_dev, nsec)),
            dma((nmpo,)),
            dma((nmpo,)),
            dma((nmpo,)),
            dma((nmpo,)),
            dma((nmpo, blk_dev)),
            dma((nmpo, blk_dev)),
            dma((nmpo, blk_dev)),
        ]
        + [pltpu.VMEM((nsec, rows, width), BF16)] * blk_dev,
        compiler_params=pltpu.CompilerParams(
            collective_id=0, has_side_effects=True, vmem_limit_bytes=24 * 2**20
        ),
    )(left_local, right_owner, right_local, left_env[0], right_env[0], mpo)


def gather_plain(nsec, nmpo, mpo, left_env, right_env, left_local, right_owner, right_local, blk_dev):
    rows, width = right_env.shape[2:]
    local_rows = rows // nmpo
    me = lax.axis_index("sector")
    first = me * blk_dev
    slots = jnp.where(right_owner == me, right_local, 0)
    wanted = [lax.dynamic_index_in_dim(right_env[0], slots[i], 0) for i in range(nsec * blk_dev)]
    outgoing = jnp.concatenate(wanted).reshape(nsec, blk_dev, rows, width)
    arrived = lax.all_to_all(outgoing, "sector", split_axis=0, concat_axis=0, tiled=True)

    own_left, own_env = [], []
    for i in range(blk_dev):
        own_left.append(
            lax.dynamic_index_in_dim(left_env[0], left_local[first + i], 0).reshape(nmpo, local_rows, rows)
        )
        own_env.append(lax.dynamic_index_in_dim(arrived[:, i], right_owner[first + i], 0))
    env_rows = blk_dev * rows
    own_env = jnp.concatenate(own_env).reshape(1, env_rows, width)
    left_rows = blk_dev * local_rows
    own_mpo = mpo[0].reshape(1, -1, width)
    packed = jnp.concatenate(
        own_left
        + [
            jnp.broadcast_to(own_env, (nmpo, env_rows, width)),
            jnp.broadcast_to(own_mpo, (nmpo,) + own_mpo.shape[1:]),
        ],
        axis=1,
    )
    got = lax.all_to_all(packed, "mpo", split_axis=0, concat_axis=0, tiled=True)
    lenv = got[:, :left_rows].reshape(nmpo, blk_dev, local_rows, rows)
    renv = got[:, left_rows : left_rows + env_rows].reshape(nmpo, blk_dev, rows, width)
    tensor = got[:, left_rows + env_rows :].reshape((nmpo,) + mpo.shape[1:])

    return lenv, renv, tensor


def body(psi, left_env, mpo, right_env, left_local, right_owner, right_local):
    blk_dev, rows, phys, width = psi.shape
    nsec = lax.axis_size("sector")
    nmpo = lax.axis_size("mpo")
    local_rows = rows // nmpo
    collect = gather if local_rows % 16 == 0 else gather_plain
    lenv, renv, tensor = collect(
        nsec, nmpo, mpo, left_env, right_env, left_local, right_owner, right_local, blk_dev
    )
    moved = jnp.einsum("wkml,klpr->kmwpr", lenv, psi, preferred_element_type=F32).astype(BF16)
    mixed = jnp.einsum("wvqp,kmwpr->kmqvr", tensor, moved, preferred_element_type=F32).astype(BF16)
    result = jnp.einsum("kmqvr,vktr->kmqt", mixed, renv, preferred_element_type=F32).astype(BF16)
    return result.reshape(blk_dev, local_rows * phys * width)


def solution(mesh):
    placed = (
        P(("groups", "sector"), None, None, None),
        P("mpo", ("groups", "sector"), None, None),
        P(("groups", "mpo"), None, None, None),
        P("mpo", ("groups", "sector"), None, None),
        P("groups"),
        P("groups"),
        P("groups"),
    )
    return jax.shard_map(
        body, mesh=mesh, in_specs=placed, out_specs=P(("groups", "sector"), "mpo"), check_vma=False
    )
```

```python
import functools

import jax
import jax.numpy as jnp
from jax import lax
from jax.experimental import pallas as pl
from jax.experimental.pallas import tpu as pltpu
from jax.sharding import PartitionSpec as P

F32 = jnp.float32
BF16 = jnp.bfloat16
MESH = pl.DeviceIdType.MESH


def exchange(
    nsec,
    nmpo,
    left_local_hbm,
    right_owner_hbm,
    right_local_hbm,
    left_env_hbm,
    right_env_hbm,
    mpo,
    lenv,
    renv,
    tensor,
    left_local,
    right_owner,
    right_local,
    left_env,
    right_env,
    load_sem,
    to_sector,
    to_mpo,
    sector_send,
    sector_recv,
    left_send,
    left_recv,
    tensor_send,
    tensor_recv,
    up_send,
    down_send,
    line_recv,
    *from_sector,
):
    blk_dev, local_rows = lenv.shape[1], lenv.shape[2]
    me = lax.axis_index("sector")
    z = lax.axis_index("mpo")
    loads = [
        pltpu.make_async_copy(src, dst, load_sem.at[i])
        for i, (src, dst) in enumerate(
            (
                (right_local_hbm, right_local),
                (right_env_hbm.at[0], right_env),
                (left_local_hbm, left_local),
                (left_env_hbm.at[0], left_env),
                (right_owner_hbm, right_owner),
                (mpo.at[0], tensor.at[z]),
            )
        )
    ]
    for load in loads:
        load.start()
    barrier = pltpu.get_barrier_semaphore()
    for d in range(1, nsec):
        pl.semaphore_signal(barrier, inc=1, device_id={"sector": lax.rem(me + d, nsec)}, device_id_type=MESH)
    for d in range(1, nmpo):
        pl.semaphore_signal(barrier, inc=1, device_id={"mpo": lax.rem(z + d, nmpo)}, device_id_type=MESH)

    loads[0].wait()
    loads[1].wait()
    for k in range(blk_dev):
        for t in range(nsec):
            to_sector[k, t] = right_env[right_local[t * blk_dev + k]]
    pl.semaphore_wait(barrier, nsec + nmpo - 2)

    def sector_copy(k, d):
        peer = lax.rem(me + d, nsec)
        return pltpu.make_async_remote_copy(
            src_ref=to_sector.at[k, peer],
            dst_ref=from_sector[k].at[me],
            send_sem=sector_send.at[k, d],
            recv_sem=sector_recv.at[k, d],
            device_id={"sector": peer},
            device_id_type=MESH,
        )

    def left_copy(d):
        peer = lax.rem(z + d, nmpo)
        return pltpu.make_async_remote_copy(
            src_ref=to_mpo.at[peer],
            dst_ref=lenv.at[z],
            send_sem=left_send.at[d],
            recv_sem=left_recv.at[d],
            device_id={"mpo": peer},
            device_id_type=MESH,
        )

    def tensor_copy(d):
        return pltpu.make_async_remote_copy(
            src_ref=mpo.at[0],
            dst_ref=tensor.at[z],
            send_sem=tensor_send.at[d],
            recv_sem=tensor_recv.at[d],
            device_id={"mpo": lax.rem(z + d, nmpo)},
            device_id_type=MESH,
        )

    def line_copy(origin, k, up):
        sems = up_send if up else down_send
        return pltpu.make_async_remote_copy(
            src_ref=renv.at[origin, k],
            dst_ref=renv.at[origin, k],
            send_sem=sems.at[origin, k],
            recv_sem=line_recv.at[origin, k],
            device_id={"mpo": z + 1 if up else z - 1},
            device_id_type=MESH,
        )

    for k in range(blk_dev):
        for d in range(1, nsec):
            sector_copy(k, d).start()
    for d in range(1, nmpo):
        tensor_copy(d).start()
    loads[2].wait()
    loads[3].wait()
    for k in range(blk_dev):
        picked = left_env[left_local[me * blk_dev + k]]
        for j in range(nmpo):
            to_mpo[j, k] = picked[j * local_rows : (j + 1) * local_rows]
    for d in range(1, nmpo):
        left_copy(d).start()
    lenv[z] = to_mpo[z]
    loads[4].wait()
    loads[5].wait()

    for k in range(blk_dev):
        from_sector[k][me] = to_sector[k, me]
        for d in range(1, nsec):
            sector_copy(k, d).wait_recv()
        renv[z, k] = from_sector[k][right_owner[me * blk_dev + k]]

        @pl.when(z < nmpo - 1)
        def _():
            line_copy(z, k, True).start()

        @pl.when(z > 0)
        def _():
            line_copy(z, k, False).start()

    for d in range(1, nmpo):
        for k in range(blk_dev):

            @pl.when(z - d >= 0)
            def _():
                line_copy(z - d, k, True).wait_recv()

                @pl.when(z < nmpo - 1)
                def _():
                    line_copy(z - d, k, True).start()

            @pl.when(z + d < nmpo)
            def _():
                line_copy(z + d, k, False).wait_recv()

                @pl.when(z > 0)
                def _():
                    line_copy(z + d, k, False).start()

    for d in range(1, nmpo):
        left_copy(d).wait()
        tensor_copy(d).wait()
    for k in range(blk_dev):
        for d in range(1, nsec):
            sector_copy(k, d).wait_send()
        for d in range(nmpo):

            @pl.when((z < nmpo - 1) & (z - d >= 0))
            def _():
                line_copy(z - d, k, True).wait_send()

            @pl.when((z > 0) & (z + d < nmpo))
            def _():
                line_copy(z + d, k, False).wait_send()


def gather(nsec, nmpo, mpo, left_env, right_env, left_local, right_owner, right_local, blk_dev):
    rows, width = right_env.shape[2:]
    local_rows = rows // nmpo
    vmem = pl.BlockSpec(memory_space=pltpu.VMEM)
    hbm = pl.BlockSpec(memory_space=pl.ANY)
    dma = pltpu.SemaphoreType.DMA
    return pl.pallas_call(
        functools.partial(exchange, nsec, nmpo),
        out_shape=(
            jax.ShapeDtypeStruct((nmpo, blk_dev, local_rows, rows), BF16),
            jax.ShapeDtypeStruct((nmpo, blk_dev, rows, width), BF16),
            jax.ShapeDtypeStruct((nmpo,) + mpo.shape[1:], BF16),
        ),
        in_specs=[hbm] * 6,
        out_specs=(vmem,) * 3,
        scratch_shapes=[
            pltpu.SMEM(left_local.shape, left_local.dtype),
            pltpu.SMEM(right_owner.shape, right_owner.dtype),
            pltpu.SMEM(right_local.shape, right_local.dtype),
            pltpu.VMEM(left_env.shape[1:], BF16),
            pltpu.VMEM(right_env.shape[1:], BF16),
            dma((6,)),
            pltpu.VMEM((blk_dev, nsec, rows, width), BF16),
            pltpu.VMEM((nmpo, blk_dev, local_rows, rows), BF16),
            dma((blk_dev, nsec)),
            dma((blk_dev, nsec)),
            dma((nmpo,)),
            dma((nmpo,)),
            dma((nmpo,)),
            dma((nmpo,)),
            dma((nmpo, blk_dev)),
            dma((nmpo, blk_dev)),
            dma((nmpo, blk_dev)),
        ]
        + [pltpu.VMEM((nsec, rows, width), BF16)] * blk_dev,
        compiler_params=pltpu.CompilerParams(
            collective_id=0, has_side_effects=True, vmem_limit_bytes=40 * 2**20
        ),
    )(left_local, right_owner, right_local, left_env, right_env, mpo)


def gather_plain(nsec, nmpo, mpo, left_env, right_env, left_local, right_owner, right_local, blk_dev):
    rows, width = right_env.shape[2:]
    local_rows = rows // nmpo
    me = lax.axis_index("sector")
    first = me * blk_dev
    slots = jnp.where(right_owner == me, right_local, 0)
    wanted = [lax.dynamic_index_in_dim(right_env[0], slots[i], 0) for i in range(nsec * blk_dev)]
    outgoing = jnp.concatenate(wanted).reshape(nsec, blk_dev, rows, width)
    arrived = lax.all_to_all(outgoing, "sector", split_axis=0, concat_axis=0, tiled=True)

    own_left, own_env = [], []
    for i in range(blk_dev):
        own_left.append(
            lax.dynamic_index_in_dim(left_env[0], left_local[first + i], 0).reshape(nmpo, local_rows, rows)
        )
        own_env.append(lax.dynamic_index_in_dim(arrived[:, i], right_owner[first + i], 0))
    env_rows = blk_dev * rows
    own_env = jnp.concatenate(own_env).reshape(1, env_rows, width)
    left_rows = blk_dev * local_rows
    own_mpo = mpo[0].reshape(1, -1, width)
    packed = jnp.concatenate(
        own_left
        + [
            jnp.broadcast_to(own_env, (nmpo, env_rows, width)),
            jnp.broadcast_to(own_mpo, (nmpo,) + own_mpo.shape[1:]),
        ],
        axis=1,
    )
    got = lax.all_to_all(packed, "mpo", split_axis=0, concat_axis=0, tiled=True)
    lenv = got[:, :left_rows].reshape(nmpo, blk_dev, local_rows, rows)
    renv = got[:, left_rows : left_rows + env_rows].reshape(nmpo, blk_dev, rows, width)
    tensor = got[:, left_rows + env_rows :].reshape((nmpo,) + mpo.shape[1:])

    return lenv, renv, tensor


def body(psi, left_env, mpo, right_env, left_local, right_owner, right_local):
    blk_dev, rows, phys, width = psi.shape
    nsec = lax.axis_size("sector")
    nmpo = lax.axis_size("mpo")
    local_rows = rows // nmpo
    collect = gather if local_rows % 16 == 0 else gather_plain
    lenv, renv, tensor = collect(
        nsec, nmpo, mpo, left_env, right_env, left_local, right_owner, right_local, blk_dev
    )
    moved = jnp.einsum("wkml,klpr->kmwpr", lenv, psi, preferred_element_type=F32).astype(BF16)
    mixed = jnp.einsum("wvqp,kmwpr->kmqvr", tensor, moved, preferred_element_type=F32).astype(BF16)
    result = jnp.einsum("kmqvr,vktr->kmqt", mixed, renv, preferred_element_type=F32).astype(BF16)
    return result.reshape(blk_dev, local_rows * phys * width)


def solution(mesh):
    placed = (
        P(("groups", "sector"), None, None, None),
        P("mpo", ("groups", "sector"), None, None),
        P(("groups", "mpo"), None, None, None),
        P("mpo", ("groups", "sector"), None, None),
        P("groups"),
        P("groups"),
        P("groups"),
    )
    return jax.shard_map(
        body, mesh=mesh, in_specs=placed, out_specs=P(("groups", "sector"), "mpo"), check_vma=False
    )
```

```python
import functools

import jax
import jax.numpy as jnp
from jax import lax
from jax.experimental import pallas as pl
from jax.experimental.pallas import tpu as pltpu
from jax.sharding import PartitionSpec as P

F32 = jnp.float32
BF16 = jnp.bfloat16
MESH = pl.DeviceIdType.MESH


def exchange(
    nsec,
    nmpo,
    left_local_hbm,
    right_owner_hbm,
    right_local_hbm,
    left_env_hbm,
    right_env_hbm,
    mpo,
    lenv,
    renv,
    tensor,
    left_local,
    right_owner,
    right_local,
    left_env,
    right_env,
    load_sem,
    to_sector,
    to_mpo,
    sector_send,
    sector_recv,
    left_send,
    left_recv,
    tensor_send,
    tensor_recv,
    up_send,
    down_send,
    line_recv,
    *from_sector,
):
    blk_dev, local_rows = lenv.shape[1], lenv.shape[2]
    piece = from_sector[0].shape[1]
    cuts = to_sector.shape[2] // piece
    chunks = blk_dev * cuts
    me = lax.axis_index("sector")
    z = lax.axis_index("mpo")
    barrier = pltpu.get_barrier_semaphore()
    for d in range(1, nsec):
        pl.semaphore_signal(barrier, inc=1, device_id={"sector": lax.rem(me + d, nsec)}, device_id_type=MESH)
    for d in range(1, nmpo):
        pl.semaphore_signal(barrier, inc=1, device_id={"mpo": lax.rem(z + d, nmpo)}, device_id_type=MESH)

    loads = [
        pltpu.make_async_copy(src, dst, load_sem.at[i])
        for i, (src, dst) in enumerate(
            (
                (right_local_hbm, right_local),
                (right_env_hbm.at[0], right_env),
                (left_local_hbm, left_local),
                (left_env_hbm.at[0], left_env),
                (right_owner_hbm, right_owner),
                (mpo.at[0], tensor.at[z]),
            )
        )
    ]
    for load in loads:
        load.start()
    loads[0].wait()
    loads[1].wait()
    for k in range(blk_dev):
        for t in range(nsec):
            to_sector[k, t] = right_env[right_local[t * blk_dev + k]]
    pl.semaphore_wait(barrier, nsec + nmpo - 2)

    def span(c):
        return pl.ds(c % cuts * piece, piece)

    def sector_copy(c, d):
        peer = lax.rem(me + d, nsec)
        return pltpu.make_async_remote_copy(
            src_ref=to_sector.at[c // cuts, peer, span(c)],
            dst_ref=from_sector[c].at[me],
            send_sem=sector_send.at[c, d],
            recv_sem=sector_recv.at[c, d],
            device_id={"sector": peer},
            device_id_type=MESH,
        )

    def left_copy(d):
        peer = lax.rem(z + d, nmpo)
        return pltpu.make_async_remote_copy(
            src_ref=to_mpo.at[peer],
            dst_ref=lenv.at[z],
            send_sem=left_send.at[d],
            recv_sem=left_recv.at[d],
            device_id={"mpo": peer},
            device_id_type=MESH,
        )

    def tensor_copy(d):
        return pltpu.make_async_remote_copy(
            src_ref=mpo.at[0],
            dst_ref=tensor.at[z],
            send_sem=tensor_send.at[d],
            recv_sem=tensor_recv.at[d],
            device_id={"mpo": lax.rem(z + d, nmpo)},
            device_id_type=MESH,
        )

    def line_copy(origin, c, up):
        sems = up_send if up else down_send
        return pltpu.make_async_remote_copy(
            src_ref=renv.at[origin, c // cuts, span(c)],
            dst_ref=renv.at[origin, c // cuts, span(c)],
            send_sem=sems.at[origin, c],
            recv_sem=line_recv.at[origin, c],
            device_id={"mpo": z + 1 if up else z - 1},
            device_id_type=MESH,
        )

    for c in range(chunks):
        for d in range(1, nsec):
            sector_copy(c, d).start()
    for d in range(1, nmpo):
        tensor_copy(d).start()
    loads[2].wait()
    loads[3].wait()
    for k in range(blk_dev):
        picked = left_env[left_local[me * blk_dev + k]]
        for j in range(nmpo):
            to_mpo[j, k] = picked[j * local_rows : (j + 1) * local_rows]
    for d in range(1, nmpo):
        left_copy(d).start()
    lenv[z] = to_mpo[z]
    loads[4].wait()
    loads[5].wait()

    for c in range(chunks):
        from_sector[c][me] = to_sector[c // cuts, me, span(c)]
        for d in range(1, nsec):
            sector_copy(c, d).wait_recv()
        renv[z, c // cuts, span(c)] = from_sector[c][right_owner[me * blk_dev + c // cuts]]

        @pl.when(z < nmpo - 1)
        def _():
            line_copy(z, c, True).start()

        @pl.when(z > 0)
        def _():
            line_copy(z, c, False).start()

    for d in range(1, nmpo):
        for c in range(chunks):

            @pl.when(z - d >= 0)
            def _():
                line_copy(z - d, c, True).wait_recv()

                @pl.when(z < nmpo - 1)
                def _():
                    line_copy(z - d, c, True).start()

            @pl.when(z + d < nmpo)
            def _():
                line_copy(z + d, c, False).wait_recv()

                @pl.when(z > 0)
                def _():
                    line_copy(z + d, c, False).start()

    for d in range(1, nmpo):
        left_copy(d).wait()
        tensor_copy(d).wait()
    for c in range(chunks):
        for d in range(1, nsec):
            sector_copy(c, d).wait_send()
        for d in range(nmpo):

            @pl.when((z < nmpo - 1) & (z - d >= 0))
            def _():
                line_copy(z - d, c, True).wait_send()

            @pl.when((z > 0) & (z + d < nmpo))
            def _():
                line_copy(z + d, c, False).wait_send()


def gather(nsec, nmpo, mpo, left_env, right_env, left_local, right_owner, right_local, blk_dev):
    rows, width = right_env.shape[2:]
    local_rows = rows // nmpo
    cuts = 2 if rows % 32 == 0 else 1
    chunks = blk_dev * cuts
    vmem = pl.BlockSpec(memory_space=pltpu.VMEM)
    hbm = pl.BlockSpec(memory_space=pltpu.HBM)
    dma = pltpu.SemaphoreType.DMA
    return pl.pallas_call(
        functools.partial(exchange, nsec, nmpo),
        out_shape=(
            jax.ShapeDtypeStruct((nmpo, blk_dev, local_rows, rows), BF16),
            jax.ShapeDtypeStruct((nmpo, blk_dev, rows, width), BF16),
            jax.ShapeDtypeStruct((nmpo,) + mpo.shape[1:], BF16),
        ),
        in_specs=[hbm] * 6,
        out_specs=(vmem,) * 3,
        scratch_shapes=[
            pltpu.SMEM(left_local.shape, left_local.dtype),
            pltpu.SMEM(right_owner.shape, right_owner.dtype),
            pltpu.SMEM(right_local.shape, right_local.dtype),
            pltpu.VMEM(left_env.shape[1:], BF16),
            pltpu.VMEM(right_env.shape[1:], BF16),
            dma((6,)),
            pltpu.VMEM((blk_dev, nsec, rows, width), BF16),
            pltpu.VMEM((nmpo, blk_dev, local_rows, rows), BF16),
            dma((chunks, nsec)),
            dma((chunks, nsec)),
            dma((nmpo,)),
            dma((nmpo,)),
            dma((nmpo,)),
            dma((nmpo,)),
            dma((nmpo, chunks)),
            dma((nmpo, chunks)),
            dma((nmpo, chunks)),
        ]
        + [pltpu.VMEM((nsec, rows // cuts, width), BF16)] * chunks,
        compiler_params=pltpu.CompilerParams(
            collective_id=0, has_side_effects=True, vmem_limit_bytes=60 * 2**20
        ),
    )(left_local, right_owner, right_local, left_env, right_env, mpo)


def gather_plain(nsec, nmpo, mpo, left_env, right_env, left_local, right_owner, right_local, blk_dev):
    rows, width = right_env.shape[2:]
    local_rows = rows // nmpo
    me = lax.axis_index("sector")
    first = me * blk_dev
    slots = jnp.where(right_owner == me, right_local, 0)
    wanted = [lax.dynamic_index_in_dim(right_env[0], slots[i], 0) for i in range(nsec * blk_dev)]
    outgoing = jnp.concatenate(wanted).reshape(nsec, blk_dev, rows, width)
    arrived = lax.all_to_all(outgoing, "sector", split_axis=0, concat_axis=0, tiled=True)

    own_left, own_env = [], []
    for i in range(blk_dev):
        own_left.append(
            lax.dynamic_index_in_dim(left_env[0], left_local[first + i], 0).reshape(nmpo, local_rows, rows)
        )
        own_env.append(lax.dynamic_index_in_dim(arrived[:, i], right_owner[first + i], 0))
    env_rows = blk_dev * rows
    own_env = jnp.concatenate(own_env).reshape(1, env_rows, width)
    left_rows = blk_dev * local_rows
    own_mpo = mpo[0].reshape(1, -1, width)
    packed = jnp.concatenate(
        own_left
        + [
            jnp.broadcast_to(own_env, (nmpo, env_rows, width)),
            jnp.broadcast_to(own_mpo, (nmpo,) + own_mpo.shape[1:]),
        ],
        axis=1,
    )
    got = lax.all_to_all(packed, "mpo", split_axis=0, concat_axis=0, tiled=True)
    lenv = got[:, :left_rows].reshape(nmpo, blk_dev, local_rows, rows)
    renv = got[:, left_rows : left_rows + env_rows].reshape(nmpo, blk_dev, rows, width)
    tensor = got[:, left_rows + env_rows :].reshape((nmpo,) + mpo.shape[1:])

    return lenv, renv, tensor


def body(psi, left_env, mpo, right_env, left_local, right_owner, right_local):
    blk_dev, rows, phys, width = psi.shape
    nsec = lax.axis_size("sector")
    nmpo = lax.axis_size("mpo")
    local_rows = rows // nmpo
    collect = gather if local_rows % 16 == 0 else gather_plain
    lenv, renv, tensor = collect(
        nsec, nmpo, mpo, left_env, right_env, left_local, right_owner, right_local, blk_dev
    )
    moved = jnp.einsum("wkml,klpr->kmwpr", lenv, psi, preferred_element_type=F32).astype(BF16)
    mixed = jnp.einsum("wvqp,kmwpr->kmqvr", tensor, moved, preferred_element_type=F32).astype(BF16)
    result = jnp.einsum("kmqvr,vktr->kmqt", mixed, renv, preferred_element_type=F32).astype(BF16)
    return result.reshape(blk_dev, local_rows * phys * width)


def solution(mesh):
    placed = (
        P(("groups", "sector"), None, None, None),
        P("mpo", ("groups", "sector"), None, None),
        P(("groups", "mpo"), None, None, None),
        P("mpo", ("groups", "sector"), None, None),
        P("groups"),
        P("groups"),
        P("groups"),
    )
    return jax.shard_map(
        body, mesh=mesh, in_specs=placed, out_specs=P(("groups", "sector"), "mpo"), check_vma=False
    )
```

```python
import functools

import jax
import jax.numpy as jnp
from jax import lax
from jax.experimental import pallas as pl
from jax.experimental.pallas import tpu as pltpu
from jax.sharding import PartitionSpec as P

F32 = jnp.float32
BF16 = jnp.bfloat16
MESH = pl.DeviceIdType.MESH


def exchange(
    nsec,
    nmpo,
    left_local_hbm,
    right_owner_hbm,
    right_local_hbm,
    left_env_hbm,
    right_env_hbm,
    mpo,
    lenv,
    renv,
    tensor,
    left_local,
    right_owner,
    right_local,
    left_env,
    right_env,
    load_sem,
    to_sector,
    to_mpo,
    sector_send,
    sector_recv,
    left_send,
    left_recv,
    tensor_send,
    tensor_recv,
    up_send,
    down_send,
    line_recv,
    *from_sector,
):
    blk_dev, local_rows = lenv.shape[1], lenv.shape[2]
    piece = from_sector[0].shape[1]
    cuts = to_sector.shape[2] // piece
    chunks = blk_dev * cuts
    me = lax.axis_index("sector")
    z = lax.axis_index("mpo")
    barrier = pltpu.get_barrier_semaphore()
    for d in range(1, nsec):
        pl.semaphore_signal(barrier, inc=1, device_id={"sector": lax.rem(me + d, nsec)}, device_id_type=MESH)
    for d in range(1, nmpo):
        pl.semaphore_signal(barrier, inc=1, device_id={"mpo": lax.rem(z + d, nmpo)}, device_id_type=MESH)

    loads = [
        pltpu.make_async_copy(src, dst, load_sem.at[i])
        for i, (src, dst) in enumerate(
            (
                (right_local_hbm, right_local),
                (right_env_hbm.at[0], right_env),
                (left_local_hbm, left_local),
                (left_env_hbm.at[0], left_env),
                (right_owner_hbm, right_owner),
                (mpo.at[0], tensor.at[z]),
            )
        )
    ]
    for load in loads:
        load.start()
    loads[0].wait()
    loads[1].wait()
    pl.semaphore_wait(barrier, nsec + nmpo - 2)

    def span(c):
        return pl.ds(c % cuts * piece, piece)

    def sector_copy(c, d):
        peer = lax.rem(me + d, nsec)
        return pltpu.make_async_remote_copy(
            src_ref=to_sector.at[c // cuts, peer, span(c)],
            dst_ref=from_sector[c].at[me],
            send_sem=sector_send.at[c, d],
            recv_sem=sector_recv.at[c, d],
            device_id={"sector": peer},
            device_id_type=MESH,
        )

    def left_copy(d):
        peer = lax.rem(z + d, nmpo)
        return pltpu.make_async_remote_copy(
            src_ref=to_mpo.at[peer],
            dst_ref=lenv.at[z],
            send_sem=left_send.at[d],
            recv_sem=left_recv.at[d],
            device_id={"mpo": peer},
            device_id_type=MESH,
        )

    def tensor_copy(d):
        return pltpu.make_async_remote_copy(
            src_ref=mpo.at[0],
            dst_ref=tensor.at[z],
            send_sem=tensor_send.at[d],
            recv_sem=tensor_recv.at[d],
            device_id={"mpo": lax.rem(z + d, nmpo)},
            device_id_type=MESH,
        )

    def line_copy(origin, c, up):
        sems = up_send if up else down_send
        return pltpu.make_async_remote_copy(
            src_ref=renv.at[origin, c // cuts, span(c)],
            dst_ref=renv.at[origin, c // cuts, span(c)],
            send_sem=sems.at[origin, c],
            recv_sem=line_recv.at[origin, c],
            device_id={"mpo": z + 1 if up else z - 1},
            device_id_type=MESH,
        )

    for k in range(blk_dev):
        for t in range(nsec):
            to_sector[k, t] = right_env[right_local[t * blk_dev + k]]
        for c in range(k * cuts, (k + 1) * cuts):
            for d in range(1, nsec):
                sector_copy(c, d).start()
    for d in range(1, nmpo):
        tensor_copy(d).start()
    loads[2].wait()
    loads[3].wait()
    for k in range(blk_dev):
        picked = left_env[left_local[me * blk_dev + k]]
        for j in range(nmpo):
            to_mpo[j, k] = picked[j * local_rows : (j + 1) * local_rows]
    for d in range(1, nmpo):
        left_copy(d).start()
    lenv[z] = to_mpo[z]
    loads[4].wait()
    loads[5].wait()

    for c in range(chunks):
        from_sector[c][me] = to_sector[c // cuts, me, span(c)]
        for d in range(1, nsec):
            sector_copy(c, d).wait_recv()
        renv[z, c // cuts, span(c)] = from_sector[c][right_owner[me * blk_dev + c // cuts]]

        @pl.when(z < nmpo - 1)
        def _():
            line_copy(z, c, True).start()

        @pl.when(z > 0)
        def _():
            line_copy(z, c, False).start()

    for d in range(1, nmpo):
        for c in range(chunks):

            @pl.when(z - d >= 0)
            def _():
                line_copy(z - d, c, True).wait_recv()

                @pl.when(z < nmpo - 1)
                def _():
                    line_copy(z - d, c, True).start()

            @pl.when(z + d < nmpo)
            def _():
                line_copy(z + d, c, False).wait_recv()

                @pl.when(z > 0)
                def _():
                    line_copy(z + d, c, False).start()

    for d in range(1, nmpo):
        left_copy(d).wait()
        tensor_copy(d).wait()
    for c in range(chunks):
        for d in range(1, nsec):
            sector_copy(c, d).wait_send()
        for d in range(nmpo):

            @pl.when((z < nmpo - 1) & (z - d >= 0))
            def _():
                line_copy(z - d, c, True).wait_send()

            @pl.when((z > 0) & (z + d < nmpo))
            def _():
                line_copy(z + d, c, False).wait_send()


def gather(nsec, nmpo, mpo, left_env, right_env, left_local, right_owner, right_local, blk_dev):
    rows, width = right_env.shape[2:]
    local_rows = rows // nmpo
    cuts = 2 if rows % 32 == 0 else 1
    chunks = blk_dev * cuts
    vmem = pl.BlockSpec(memory_space=pltpu.VMEM)
    hbm = pl.BlockSpec(memory_space=pltpu.HBM)
    dma = pltpu.SemaphoreType.DMA
    return pl.pallas_call(
        functools.partial(exchange, nsec, nmpo),
        out_shape=(
            jax.ShapeDtypeStruct((nmpo, blk_dev, local_rows, rows), BF16),
            jax.ShapeDtypeStruct((nmpo, blk_dev, rows, width), BF16),
            jax.ShapeDtypeStruct((nmpo,) + mpo.shape[1:], BF16),
        ),
        in_specs=[hbm] * 6,
        out_specs=(vmem,) * 3,
        scratch_shapes=[
            pltpu.SMEM(left_local.shape, left_local.dtype),
            pltpu.SMEM(right_owner.shape, right_owner.dtype),
            pltpu.SMEM(right_local.shape, right_local.dtype),
            pltpu.VMEM(left_env.shape[1:], BF16),
            pltpu.VMEM(right_env.shape[1:], BF16),
            dma((6,)),
            pltpu.VMEM((blk_dev, nsec, rows, width), BF16),
            pltpu.VMEM((nmpo, blk_dev, local_rows, rows), BF16),
            dma((chunks, nsec)),
            dma((chunks, nsec)),
            dma((nmpo,)),
            dma((nmpo,)),
            dma((nmpo,)),
            dma((nmpo,)),
            dma((nmpo, chunks)),
            dma((nmpo, chunks)),
            dma((nmpo, chunks)),
        ]
        + [pltpu.VMEM((nsec, rows // cuts, width), BF16)] * chunks,
        compiler_params=pltpu.CompilerParams(
            collective_id=0, has_side_effects=True, vmem_limit_bytes=63 * 2**20
        ),
    )(left_local, right_owner, right_local, left_env, right_env, mpo)


def gather_plain(nsec, nmpo, mpo, left_env, right_env, left_local, right_owner, right_local, blk_dev):
    rows, width = right_env.shape[2:]
    local_rows = rows // nmpo
    me = lax.axis_index("sector")
    first = me * blk_dev
    slots = jnp.where(right_owner == me, right_local, 0)
    wanted = [lax.dynamic_index_in_dim(right_env[0], slots[i], 0) for i in range(nsec * blk_dev)]
    outgoing = jnp.concatenate(wanted).reshape(nsec, blk_dev, rows, width)
    arrived = lax.all_to_all(outgoing, "sector", split_axis=0, concat_axis=0, tiled=True)

    own_left, own_env = [], []
    for i in range(blk_dev):
        own_left.append(
            lax.dynamic_index_in_dim(left_env[0], left_local[first + i], 0).reshape(nmpo, local_rows, rows)
        )
        own_env.append(lax.dynamic_index_in_dim(arrived[:, i], right_owner[first + i], 0))
    env_rows = blk_dev * rows
    own_env = jnp.concatenate(own_env).reshape(1, env_rows, width)
    left_rows = blk_dev * local_rows
    own_mpo = mpo[0].reshape(1, -1, width)
    packed = jnp.concatenate(
        own_left
        + [
            jnp.broadcast_to(own_env, (nmpo, env_rows, width)),
            jnp.broadcast_to(own_mpo, (nmpo,) + own_mpo.shape[1:]),
        ],
        axis=1,
    )
    got = lax.all_to_all(packed, "mpo", split_axis=0, concat_axis=0, tiled=True)
    lenv = got[:, :left_rows].reshape(nmpo, blk_dev, local_rows, rows)
    renv = got[:, left_rows : left_rows + env_rows].reshape(nmpo, blk_dev, rows, width)
    tensor = got[:, left_rows + env_rows :].reshape((nmpo,) + mpo.shape[1:])

    return lenv, renv, tensor


def body(psi, left_env, mpo, right_env, left_local, right_owner, right_local):
    blk_dev, rows, phys, width = psi.shape
    nsec = lax.axis_size("sector")
    nmpo = lax.axis_size("mpo")
    local_rows = rows // nmpo
    collect = gather if local_rows % 16 == 0 else gather_plain
    lenv, renv, tensor = collect(
        nsec, nmpo, mpo, left_env, right_env, left_local, right_owner, right_local, blk_dev
    )
    moved = jnp.einsum("wkml,klpr->kmwpr", lenv, psi, preferred_element_type=F32).astype(BF16)
    mixed = jnp.einsum("wvqp,kmwpr->kmqvr", tensor, moved, preferred_element_type=F32).astype(BF16)
    result = jnp.einsum("kmqvr,vktr->kmqt", mixed, renv, preferred_element_type=F32).astype(BF16)
    return result.reshape(blk_dev, local_rows * phys * width)


def solution(mesh):
    placed = (
        P(("groups", "sector"), None, None, None),
        P("mpo", ("groups", "sector"), None, None),
        P(("groups", "mpo"), None, None, None),
        P("mpo", ("groups", "sector"), None, None),
        P("groups"),
        P("groups"),
        P("groups"),
    )
    return jax.shard_map(
        body, mesh=mesh, in_specs=placed, out_specs=P(("groups", "sector"), "mpo"), check_vma=False
    )
```

```python
import functools

import jax
import jax.numpy as jnp
from jax import lax
from jax.experimental import pallas as pl
from jax.experimental.pallas import tpu as pltpu
from jax.sharding import PartitionSpec as P

F32 = jnp.float32
BF16 = jnp.bfloat16
MESH = pl.DeviceIdType.MESH


def exchange(
    nsec,
    nmpo,
    left_local_hbm,
    right_owner_hbm,
    right_local_hbm,
    left_env_hbm,
    right_env_hbm,
    mpo,
    lenv,
    renv,
    tensor,
    left_local,
    right_owner,
    right_local,
    left_env,
    right_env,
    load_sem,
    to_sector,
    to_mpo,
    sector_send,
    sector_recv,
    left_send,
    left_recv,
    tensor_send,
    tensor_recv,
    own_send,
    own_recv,
    *from_sector,
):
    blk_dev, local_rows = lenv.shape[1], lenv.shape[2]
    piece = from_sector[0].shape[1]
    cuts = to_sector.shape[2] // piece
    chunks = blk_dev * cuts
    me = lax.axis_index("sector")
    z = lax.axis_index("mpo")
    barrier = pltpu.get_barrier_semaphore()
    for d in range(1, nsec):
        pl.semaphore_signal(barrier, inc=1, device_id={"sector": lax.rem(me + d, nsec)}, device_id_type=MESH)
    for d in range(1, nmpo):
        pl.semaphore_signal(barrier, inc=1, device_id={"mpo": lax.rem(z + d, nmpo)}, device_id_type=MESH)

    loads = [
        pltpu.make_async_copy(src, dst, load_sem.at[i])
        for i, (src, dst) in enumerate(
            (
                (right_local_hbm, right_local),
                (right_env_hbm.at[0], right_env),
                (left_local_hbm, left_local),
                (left_env_hbm.at[0], left_env),
                (right_owner_hbm, right_owner),
                (mpo.at[0], tensor.at[z]),
            )
        )
    ]
    for load in loads:
        load.start()
    loads[0].wait()
    loads[1].wait()
    pl.semaphore_wait(barrier, nsec + nmpo - 2)

    def span(c):
        return pl.ds(c % cuts * piece, piece)

    def sector_copy(c, d):
        peer = lax.rem(me + d, nsec)
        return pltpu.make_async_remote_copy(
            src_ref=to_sector.at[c // cuts, peer, span(c)],
            dst_ref=from_sector[c].at[me],
            send_sem=sector_send.at[c, d],
            recv_sem=sector_recv.at[c, d],
            device_id={"sector": peer},
            device_id_type=MESH,
        )

    def left_copy(d):
        peer = lax.rem(z + d, nmpo)
        return pltpu.make_async_remote_copy(
            src_ref=to_mpo.at[peer],
            dst_ref=lenv.at[z],
            send_sem=left_send.at[d],
            recv_sem=left_recv.at[d],
            device_id={"mpo": peer},
            device_id_type=MESH,
        )

    def tensor_copy(d):
        return pltpu.make_async_remote_copy(
            src_ref=mpo.at[0],
            dst_ref=tensor.at[z],
            send_sem=tensor_send.at[d],
            recv_sem=tensor_recv.at[d],
            device_id={"mpo": lax.rem(z + d, nmpo)},
            device_id_type=MESH,
        )

    def own_copy(c, d):
        return pltpu.make_async_remote_copy(
            src_ref=renv.at[z, c // cuts, span(c)],
            dst_ref=renv.at[z, c // cuts, span(c)],
            send_sem=own_send.at[d, c],
            recv_sem=own_recv.at[d, c],
            device_id={"mpo": lax.rem(z + d, nmpo)},
            device_id_type=MESH,
        )

    for k in range(blk_dev):
        for t in range(nsec):
            to_sector[k, t] = right_env[right_local[t * blk_dev + k]]
        for c in range(k * cuts, (k + 1) * cuts):
            for d in range(1, nsec):
                sector_copy(c, d).start()
    for d in range(1, nmpo):
        tensor_copy(d).start()
    loads[2].wait()
    loads[3].wait()
    for k in range(blk_dev):
        picked = left_env[left_local[me * blk_dev + k]]
        for j in range(nmpo):
            to_mpo[j, k] = picked[j * local_rows : (j + 1) * local_rows]
    for d in range(1, nmpo):
        left_copy(d).start()
    lenv[z] = to_mpo[z]
    loads[4].wait()
    loads[5].wait()

    for c in range(chunks):
        from_sector[c][me] = to_sector[c // cuts, me, span(c)]
        for d in range(1, nsec):
            sector_copy(c, d).wait_recv()
        renv[z, c // cuts, span(c)] = from_sector[c][right_owner[me * blk_dev + c // cuts]]

        for d in range(1, nmpo):
            own_copy(c, d).start()

    for d in range(1, nmpo):
        left_copy(d).wait()
        tensor_copy(d).wait()
    for c in range(chunks):
        for d in range(1, nmpo):
            own_copy(c, d).wait()
        for d in range(1, nsec):
            sector_copy(c, d).wait_send()


def gather(nsec, nmpo, mpo, left_env, right_env, left_local, right_owner, right_local, blk_dev):
    rows, width = right_env.shape[2:]
    local_rows = rows // nmpo
    cuts = 2 if rows % 32 == 0 else 1
    chunks = blk_dev * cuts
    vmem = pl.BlockSpec(memory_space=pltpu.VMEM)
    hbm = pl.BlockSpec(memory_space=pltpu.HBM)
    dma = pltpu.SemaphoreType.DMA
    return pl.pallas_call(
        functools.partial(exchange, nsec, nmpo),
        out_shape=(
            jax.ShapeDtypeStruct((nmpo, blk_dev, local_rows, rows), BF16),
            jax.ShapeDtypeStruct((nmpo, blk_dev, rows, width), BF16),
            jax.ShapeDtypeStruct((nmpo,) + mpo.shape[1:], BF16),
        ),
        in_specs=[hbm] * 6,
        out_specs=(vmem,) * 3,
        scratch_shapes=[
            pltpu.SMEM(left_local.shape, left_local.dtype),
            pltpu.SMEM(right_owner.shape, right_owner.dtype),
            pltpu.SMEM(right_local.shape, right_local.dtype),
            pltpu.VMEM(left_env.shape[1:], BF16),
            pltpu.VMEM(right_env.shape[1:], BF16),
            dma((6,)),
            pltpu.VMEM((blk_dev, nsec, rows, width), BF16),
            pltpu.VMEM((nmpo, blk_dev, local_rows, rows), BF16),
            dma((chunks, nsec)),
            dma((chunks, nsec)),
            dma((nmpo,)),
            dma((nmpo,)),
            dma((nmpo,)),
            dma((nmpo,)),
            dma((nmpo, chunks)),
            dma((nmpo, chunks)),
        ]
        + [pltpu.VMEM((nsec, rows // cuts, width), BF16)] * chunks,
        compiler_params=pltpu.CompilerParams(
            collective_id=0, has_side_effects=True, vmem_limit_bytes=63 * 2**20
        ),
    )(left_local, right_owner, right_local, left_env, right_env, mpo)


def gather_plain(nsec, nmpo, mpo, left_env, right_env, left_local, right_owner, right_local, blk_dev):
    rows, width = right_env.shape[2:]
    local_rows = rows // nmpo
    me = lax.axis_index("sector")
    first = me * blk_dev
    slots = jnp.where(right_owner == me, right_local, 0)
    wanted = [lax.dynamic_index_in_dim(right_env[0], slots[i], 0) for i in range(nsec * blk_dev)]
    outgoing = jnp.concatenate(wanted).reshape(nsec, blk_dev, rows, width)
    arrived = lax.all_to_all(outgoing, "sector", split_axis=0, concat_axis=0, tiled=True)

    own_left, own_env = [], []
    for i in range(blk_dev):
        own_left.append(
            lax.dynamic_index_in_dim(left_env[0], left_local[first + i], 0).reshape(nmpo, local_rows, rows)
        )
        own_env.append(lax.dynamic_index_in_dim(arrived[:, i], right_owner[first + i], 0))
    env_rows = blk_dev * rows
    own_env = jnp.concatenate(own_env).reshape(1, env_rows, width)
    left_rows = blk_dev * local_rows
    own_mpo = mpo[0].reshape(1, -1, width)
    packed = jnp.concatenate(
        own_left
        + [
            jnp.broadcast_to(own_env, (nmpo, env_rows, width)),
            jnp.broadcast_to(own_mpo, (nmpo,) + own_mpo.shape[1:]),
        ],
        axis=1,
    )
    got = lax.all_to_all(packed, "mpo", split_axis=0, concat_axis=0, tiled=True)
    lenv = got[:, :left_rows].reshape(nmpo, blk_dev, local_rows, rows)
    renv = got[:, left_rows : left_rows + env_rows].reshape(nmpo, blk_dev, rows, width)
    tensor = got[:, left_rows + env_rows :].reshape((nmpo,) + mpo.shape[1:])

    return lenv, renv, tensor


def body(psi, left_env, mpo, right_env, left_local, right_owner, right_local):
    blk_dev, rows, phys, width = psi.shape
    nsec = lax.axis_size("sector")
    nmpo = lax.axis_size("mpo")
    local_rows = rows // nmpo
    collect = gather if local_rows % 16 == 0 else gather_plain
    lenv, renv, tensor = collect(
        nsec, nmpo, mpo, left_env, right_env, left_local, right_owner, right_local, blk_dev
    )
    moved = jnp.einsum("wkml,klpr->kmwpr", lenv, psi, preferred_element_type=F32).astype(BF16)
    mixed = jnp.einsum("wvqp,kmwpr->kmqvr", tensor, moved, preferred_element_type=F32).astype(BF16)
    result = jnp.einsum("kmqvr,vktr->kmqt", mixed, renv, preferred_element_type=F32).astype(BF16)
    return result.reshape(blk_dev, local_rows * phys * width)


def solution(mesh):
    placed = (
        P(("groups", "sector"), None, None, None),
        P("mpo", ("groups", "sector"), None, None),
        P(("groups", "mpo"), None, None, None),
        P("mpo", ("groups", "sector"), None, None),
        P("groups"),
        P("groups"),
        P("groups"),
    )
    return jax.shard_map(
        body, mesh=mesh, in_specs=placed, out_specs=P(("groups", "sector"), "mpo"), check_vma=False
    )
```

```python
import functools

import jax
import jax.numpy as jnp
from jax import lax
from jax.experimental import pallas as pl
from jax.experimental.pallas import tpu as pltpu
from jax.sharding import PartitionSpec as P

F32 = jnp.float32
BF16 = jnp.bfloat16
MESH = pl.DeviceIdType.MESH


def exchange(
    nsec,
    nmpo,
    left_local_hbm,
    right_owner_hbm,
    right_local_hbm,
    left_env_hbm,
    right_env_hbm,
    mpo,
    lenv,
    renv,
    tensor,
    left_local,
    right_owner,
    right_local,
    left_env,
    right_env,
    load_sem,
    to_sector,
    to_mpo,
    sector_send,
    sector_recv,
    left_send,
    left_recv,
    tensor_send,
    tensor_recv,
    own_send,
    own_recv,
    far_send,
    *from_sector,
):
    blk_dev, local_rows = lenv.shape[1], lenv.shape[2]
    piece = from_sector[0].shape[1]
    cuts = to_sector.shape[2] // piece
    chunks = blk_dev * cuts
    me = lax.axis_index("sector")
    z = lax.axis_index("mpo")
    barrier = pltpu.get_barrier_semaphore()
    for d in range(1, nsec):
        pl.semaphore_signal(barrier, inc=1, device_id={"sector": lax.rem(me + d, nsec)}, device_id_type=MESH)
    for d in range(1, nmpo):
        pl.semaphore_signal(barrier, inc=1, device_id={"mpo": lax.rem(z + d, nmpo)}, device_id_type=MESH)

    loads = [
        pltpu.make_async_copy(src, dst, load_sem.at[i])
        for i, (src, dst) in enumerate(
            (
                (right_local_hbm, right_local),
                (right_env_hbm.at[0], right_env),
                (left_local_hbm, left_local),
                (left_env_hbm.at[0], left_env),
                (right_owner_hbm, right_owner),
                (mpo.at[0], tensor.at[z]),
            )
        )
    ]
    for load in loads:
        load.start()
    loads[0].wait()
    loads[1].wait()
    pl.semaphore_wait(barrier, nsec + nmpo - 2)

    def span(c):
        return pl.ds(c % cuts * piece, piece)

    def sector_copy(c, d):
        peer = lax.rem(me + d, nsec)
        return pltpu.make_async_remote_copy(
            src_ref=to_sector.at[c // cuts, peer, span(c)],
            dst_ref=from_sector[c].at[me],
            send_sem=sector_send.at[c, d],
            recv_sem=sector_recv.at[c, d],
            device_id={"sector": peer},
            device_id_type=MESH,
        )

    def left_copy(d):
        peer = lax.rem(z + d, nmpo)
        return pltpu.make_async_remote_copy(
            src_ref=to_mpo.at[peer],
            dst_ref=lenv.at[z],
            send_sem=left_send.at[d],
            recv_sem=left_recv.at[d],
            device_id={"mpo": peer},
            device_id_type=MESH,
        )

    def tensor_copy(d):
        return pltpu.make_async_remote_copy(
            src_ref=mpo.at[0],
            dst_ref=tensor.at[z],
            send_sem=tensor_send.at[d],
            recv_sem=tensor_recv.at[d],
            device_id={"mpo": lax.rem(z + d, nmpo)},
            device_id_type=MESH,
        )

    def own_copy(c, d):
        return pltpu.make_async_remote_copy(
            src_ref=renv.at[z, c // cuts, span(c)],
            dst_ref=renv.at[z, c // cuts, span(c)],
            send_sem=own_send.at[d, c],
            recv_sem=own_recv.at[d, c],
            device_id={"mpo": lax.rem(z + d, nmpo)},
            device_id_type=MESH,
        )

    relay = nmpo == 4
    order = (2, 1, 3) if relay else tuple(range(1, nmpo))

    def near(d):
        if relay and d == 3:
            return z > 0
        if relay and d == 1:
            return z < nmpo - 1
        return z >= 0

    def far_copy(c):
        origin = lax.rem(z + 2, nmpo)
        target = nmpo - 1 - origin
        return pltpu.make_async_remote_copy(
            src_ref=renv.at[origin, c // cuts, span(c)],
            dst_ref=renv.at[origin, c // cuts, span(c)],
            send_sem=far_send.at[c],
            recv_sem=own_recv.at[lax.rem(target - origin + nmpo, nmpo), c],
            device_id={"mpo": target},
            device_id_type=MESH,
        )

    for k in range(blk_dev):
        for t in range(nsec):
            to_sector[k, t] = right_env[right_local[t * blk_dev + k]]
        for c in range(k * cuts, (k + 1) * cuts):
            for d in range(1, nsec):
                sector_copy(c, d).start()
    for d in range(1, nmpo):
        tensor_copy(d).start()
    loads[2].wait()
    loads[3].wait()
    for k in range(blk_dev):
        picked = left_env[left_local[me * blk_dev + k]]
        for j in range(nmpo):
            to_mpo[j, k] = picked[j * local_rows : (j + 1) * local_rows]
    for d in range(1, nmpo):
        left_copy(d).start()
    lenv[z] = to_mpo[z]
    loads[4].wait()
    loads[5].wait()

    for c in range(chunks):
        from_sector[c][me] = to_sector[c // cuts, me, span(c)]
        for d in range(1, nsec):
            sector_copy(c, d).wait_recv()
        renv[z, c // cuts, span(c)] = from_sector[c][right_owner[me * blk_dev + c // cuts]]

        for d in order:

            @pl.when(near(d))
            def _():
                own_copy(c, d).start()

    if relay:
        for c in range(chunks):
            own_copy(c, 2).wait_recv()

            @pl.when((z > 0) & (z < nmpo - 1))
            def _():
                far_copy(c).start()

    for d in range(1, nmpo):
        left_copy(d).wait()
        tensor_copy(d).wait()
    for c in range(chunks):
        for d in order:
            if not (relay and d == 2):
                own_copy(c, d).wait_recv()

            @pl.when(near(d))
            def _():
                own_copy(c, d).wait_send()

        if relay:

            @pl.when((z > 0) & (z < nmpo - 1))
            def _():
                far_copy(c).wait_send()

        for d in range(1, nsec):
            sector_copy(c, d).wait_send()


def gather(nsec, nmpo, mpo, left_env, right_env, left_local, right_owner, right_local, blk_dev):
    rows, width = right_env.shape[2:]
    local_rows = rows // nmpo
    cuts = 2 if rows % 32 == 0 else 1
    chunks = blk_dev * cuts
    vmem = pl.BlockSpec(memory_space=pltpu.VMEM)
    hbm = pl.BlockSpec(memory_space=pltpu.HBM)
    dma = pltpu.SemaphoreType.DMA
    return pl.pallas_call(
        functools.partial(exchange, nsec, nmpo),
        out_shape=(
            jax.ShapeDtypeStruct((nmpo, blk_dev, local_rows, rows), BF16),
            jax.ShapeDtypeStruct((nmpo, blk_dev, rows, width), BF16),
            jax.ShapeDtypeStruct((nmpo,) + mpo.shape[1:], BF16),
        ),
        in_specs=[hbm] * 6,
        out_specs=(vmem,) * 3,
        scratch_shapes=[
            pltpu.SMEM(left_local.shape, left_local.dtype),
            pltpu.SMEM(right_owner.shape, right_owner.dtype),
            pltpu.SMEM(right_local.shape, right_local.dtype),
            pltpu.VMEM(left_env.shape[1:], BF16),
            pltpu.VMEM(right_env.shape[1:], BF16),
            dma((6,)),
            pltpu.VMEM((blk_dev, nsec, rows, width), BF16),
            pltpu.VMEM((nmpo, blk_dev, local_rows, rows), BF16),
            dma((chunks, nsec)),
            dma((chunks, nsec)),
            dma((nmpo,)),
            dma((nmpo,)),
            dma((nmpo,)),
            dma((nmpo,)),
            dma((nmpo, chunks)),
            dma((nmpo, chunks)),
            dma((chunks,)),
        ]
        + [pltpu.VMEM((nsec, rows // cuts, width), BF16)] * chunks,
        compiler_params=pltpu.CompilerParams(
            collective_id=0, has_side_effects=True, vmem_limit_bytes=63 * 2**20
        ),
    )(left_local, right_owner, right_local, left_env, right_env, mpo)


def gather_plain(nsec, nmpo, mpo, left_env, right_env, left_local, right_owner, right_local, blk_dev):
    rows, width = right_env.shape[2:]
    local_rows = rows // nmpo
    me = lax.axis_index("sector")
    first = me * blk_dev
    slots = jnp.where(right_owner == me, right_local, 0)
    wanted = [lax.dynamic_index_in_dim(right_env[0], slots[i], 0) for i in range(nsec * blk_dev)]
    outgoing = jnp.concatenate(wanted).reshape(nsec, blk_dev, rows, width)
    arrived = lax.all_to_all(outgoing, "sector", split_axis=0, concat_axis=0, tiled=True)

    own_left, own_env = [], []
    for i in range(blk_dev):
        own_left.append(
            lax.dynamic_index_in_dim(left_env[0], left_local[first + i], 0).reshape(nmpo, local_rows, rows)
        )
        own_env.append(lax.dynamic_index_in_dim(arrived[:, i], right_owner[first + i], 0))
    env_rows = blk_dev * rows
    own_env = jnp.concatenate(own_env).reshape(1, env_rows, width)
    left_rows = blk_dev * local_rows
    own_mpo = mpo[0].reshape(1, -1, width)
    packed = jnp.concatenate(
        own_left
        + [
            jnp.broadcast_to(own_env, (nmpo, env_rows, width)),
            jnp.broadcast_to(own_mpo, (nmpo,) + own_mpo.shape[1:]),
        ],
        axis=1,
    )
    got = lax.all_to_all(packed, "mpo", split_axis=0, concat_axis=0, tiled=True)
    lenv = got[:, :left_rows].reshape(nmpo, blk_dev, local_rows, rows)
    renv = got[:, left_rows : left_rows + env_rows].reshape(nmpo, blk_dev, rows, width)
    tensor = got[:, left_rows + env_rows :].reshape((nmpo,) + mpo.shape[1:])

    return lenv, renv, tensor


def body(psi, left_env, mpo, right_env, left_local, right_owner, right_local):
    blk_dev, rows, phys, width = psi.shape
    nsec = lax.axis_size("sector")
    nmpo = lax.axis_size("mpo")
    local_rows = rows // nmpo
    collect = gather if local_rows % 16 == 0 else gather_plain
    lenv, renv, tensor = collect(
        nsec, nmpo, mpo, left_env, right_env, left_local, right_owner, right_local, blk_dev
    )
    moved = jnp.einsum("wkml,klpr->kmwpr", lenv, psi, preferred_element_type=F32).astype(BF16)
    mixed = jnp.einsum("wvqp,kmwpr->kmqvr", tensor, moved, preferred_element_type=F32).astype(BF16)
    result = jnp.einsum("kmqvr,vktr->kmqt", mixed, renv, preferred_element_type=F32).astype(BF16)
    return result.reshape(blk_dev, local_rows * phys * width)


def solution(mesh):
    placed = (
        P(("groups", "sector"), None, None, None),
        P("mpo", ("groups", "sector"), None, None),
        P(("groups", "mpo"), None, None, None),
        P("mpo", ("groups", "sector"), None, None),
        P("groups"),
        P("groups"),
        P("groups"),
    )
    return jax.shard_map(
        body, mesh=mesh, in_specs=placed, out_specs=P(("groups", "sector"), "mpo"), check_vma=False
    )
```

```python
import functools

import jax
import jax.numpy as jnp
from jax import lax
from jax.experimental import pallas as pl
from jax.experimental.pallas import tpu as pltpu
from jax.sharding import PartitionSpec as P

F32 = jnp.float32
BF16 = jnp.bfloat16
MESH = pl.DeviceIdType.MESH


def exchange(
    nsec,
    nmpo,
    left_local_hbm,
    right_owner_hbm,
    right_local_hbm,
    left_env_hbm,
    right_env_hbm,
    mpo,
    lenv,
    renv,
    tensor,
    left_local,
    right_owner,
    right_local,
    left_env,
    right_env,
    load_sem,
    to_sector,
    to_mpo,
    sector_send,
    sector_recv,
    left_send,
    left_recv,
    tensor_send,
    tensor_recv,
    own_send,
    own_recv,
    *from_sector,
):
    blk_dev, local_rows = lenv.shape[1], lenv.shape[2]
    piece = from_sector[0].shape[1]
    cuts = to_sector.shape[2] // piece
    chunks = blk_dev * cuts
    me = lax.axis_index("sector")
    z = lax.axis_index("mpo")
    barrier = pltpu.get_barrier_semaphore()
    for d in range(1, nsec):
        pl.semaphore_signal(barrier, inc=1, device_id={"sector": lax.rem(me + d, nsec)}, device_id_type=MESH)
    for d in range(1, nmpo):
        pl.semaphore_signal(barrier, inc=1, device_id={"mpo": lax.rem(z + d, nmpo)}, device_id_type=MESH)

    loads = [
        pltpu.make_async_copy(src, dst, load_sem.at[i])
        for i, (src, dst) in enumerate(
            (
                (right_local_hbm, right_local),
                (right_env_hbm.at[0], right_env),
                (left_local_hbm, left_local),
                (left_env_hbm.at[0], left_env),
                (right_owner_hbm, right_owner),
                (mpo.at[0], tensor.at[z]),
            )
        )
    ]
    for load in loads:
        load.start()
    loads[0].wait()
    loads[1].wait()
    pl.semaphore_wait(barrier, nsec + nmpo - 2)

    def span(c):
        return pl.ds(c % cuts * piece, piece)

    def sector_copy(c, d):
        peer = lax.rem(me + d, nsec)
        return pltpu.make_async_remote_copy(
            src_ref=to_sector.at[c // cuts, peer, span(c)],
            dst_ref=from_sector[c].at[me],
            send_sem=sector_send.at[c, d],
            recv_sem=sector_recv.at[c, d],
            device_id={"sector": peer},
            device_id_type=MESH,
        )

    def left_copy(d):
        peer = lax.rem(z + d, nmpo)
        return pltpu.make_async_remote_copy(
            src_ref=to_mpo.at[peer],
            dst_ref=lenv.at[z],
            send_sem=left_send.at[d],
            recv_sem=left_recv.at[d],
            device_id={"mpo": peer},
            device_id_type=MESH,
        )

    def tensor_copy(d):
        return pltpu.make_async_remote_copy(
            src_ref=mpo.at[0],
            dst_ref=tensor.at[z],
            send_sem=tensor_send.at[d],
            recv_sem=tensor_recv.at[d],
            device_id={"mpo": lax.rem(z + d, nmpo)},
            device_id_type=MESH,
        )

    def own_copy(c, d):
        return pltpu.make_async_remote_copy(
            src_ref=renv.at[z, c // cuts, span(c)],
            dst_ref=renv.at[z, c // cuts, span(c)],
            send_sem=own_send.at[d, c],
            recv_sem=own_recv.at[d, c],
            device_id={"mpo": lax.rem(z + d, nmpo)},
            device_id_type=MESH,
        )

    for k in range(blk_dev):
        for t in range(nsec):
            to_sector[k, t] = right_env[right_local[t * blk_dev + k]]
        for c in range(k * cuts, (k + 1) * cuts):
            for d in range(1, nsec):
                sector_copy(c, d).start()
    for d in range(1, nmpo):
        tensor_copy(d).start()
    loads[2].wait()
    loads[3].wait()
    for k in range(blk_dev):
        picked = left_env[left_local[me * blk_dev + k]]
        for j in range(nmpo):
            to_mpo[j, k] = picked[j * local_rows : (j + 1) * local_rows]
    for d in range(1, nmpo):
        left_copy(d).start()
    lenv[z] = to_mpo[z]
    loads[4].wait()
    loads[5].wait()

    for c in range(chunks):
        from_sector[c][me] = to_sector[c // cuts, me, span(c)]
        for d in range(1, nsec):
            sector_copy(c, d).wait_recv()
        renv[z, c // cuts, span(c)] = from_sector[c][right_owner[me * blk_dev + c // cuts]]

        for d in range(1, nmpo):
            own_copy(c, d).start()

    for d in range(1, nmpo):
        left_copy(d).wait()
        tensor_copy(d).wait()
    for c in range(chunks):
        for d in range(1, nmpo):
            own_copy(c, d).wait()
        for d in range(1, nsec):
            sector_copy(c, d).wait_send()


def gather(nsec, nmpo, mpo, left_env, right_env, left_local, right_owner, right_local, blk_dev):
    rows, width = right_env.shape[2:]
    local_rows = rows // nmpo
    cuts = 1
    chunks = blk_dev * cuts
    vmem = pl.BlockSpec(memory_space=pltpu.VMEM)
    hbm = pl.BlockSpec(memory_space=pltpu.HBM)
    dma = pltpu.SemaphoreType.DMA
    return pl.pallas_call(
        functools.partial(exchange, nsec, nmpo),
        out_shape=(
            jax.ShapeDtypeStruct((nmpo, blk_dev, local_rows, rows), BF16),
            jax.ShapeDtypeStruct((nmpo, blk_dev, rows, width), BF16),
            jax.ShapeDtypeStruct((nmpo,) + mpo.shape[1:], BF16),
        ),
        in_specs=[hbm] * 6,
        out_specs=(vmem,) * 3,
        scratch_shapes=[
            pltpu.SMEM(left_local.shape, left_local.dtype),
            pltpu.SMEM(right_owner.shape, right_owner.dtype),
            pltpu.SMEM(right_local.shape, right_local.dtype),
            pltpu.VMEM(left_env.shape[1:], BF16),
            pltpu.VMEM(right_env.shape[1:], BF16),
            dma((6,)),
            pltpu.VMEM((blk_dev, nsec, rows, width), BF16),
            pltpu.VMEM((nmpo, blk_dev, local_rows, rows), BF16),
            dma((chunks, nsec)),
            dma((chunks, nsec)),
            dma((nmpo,)),
            dma((nmpo,)),
            dma((nmpo,)),
            dma((nmpo,)),
            dma((nmpo, chunks)),
            dma((nmpo, chunks)),
        ]
        + [pltpu.VMEM((nsec, rows // cuts, width), BF16)] * chunks,
        compiler_params=pltpu.CompilerParams(
            collective_id=0, has_side_effects=True, vmem_limit_bytes=63 * 2**20
        ),
    )(left_local, right_owner, right_local, left_env, right_env, mpo)


def gather_plain(nsec, nmpo, mpo, left_env, right_env, left_local, right_owner, right_local, blk_dev):
    rows, width = right_env.shape[2:]
    local_rows = rows // nmpo
    me = lax.axis_index("sector")
    first = me * blk_dev
    slots = jnp.where(right_owner == me, right_local, 0)
    wanted = [lax.dynamic_index_in_dim(right_env[0], slots[i], 0) for i in range(nsec * blk_dev)]
    outgoing = jnp.concatenate(wanted).reshape(nsec, blk_dev, rows, width)
    arrived = lax.all_to_all(outgoing, "sector", split_axis=0, concat_axis=0, tiled=True)

    own_left, own_env = [], []
    for i in range(blk_dev):
        own_left.append(
            lax.dynamic_index_in_dim(left_env[0], left_local[first + i], 0).reshape(nmpo, local_rows, rows)
        )
        own_env.append(lax.dynamic_index_in_dim(arrived[:, i], right_owner[first + i], 0))
    env_rows = blk_dev * rows
    own_env = jnp.concatenate(own_env).reshape(1, env_rows, width)
    left_rows = blk_dev * local_rows
    own_mpo = mpo[0].reshape(1, -1, width)
    packed = jnp.concatenate(
        own_left
        + [
            jnp.broadcast_to(own_env, (nmpo, env_rows, width)),
            jnp.broadcast_to(own_mpo, (nmpo,) + own_mpo.shape[1:]),
        ],
        axis=1,
    )
    got = lax.all_to_all(packed, "mpo", split_axis=0, concat_axis=0, tiled=True)
    lenv = got[:, :left_rows].reshape(nmpo, blk_dev, local_rows, rows)
    renv = got[:, left_rows : left_rows + env_rows].reshape(nmpo, blk_dev, rows, width)
    tensor = got[:, left_rows + env_rows :].reshape((nmpo,) + mpo.shape[1:])

    return lenv, renv, tensor


def body(psi, left_env, mpo, right_env, left_local, right_owner, right_local):
    blk_dev, rows, phys, width = psi.shape
    nsec = lax.axis_size("sector")
    nmpo = lax.axis_size("mpo")
    local_rows = rows // nmpo
    collect = gather if local_rows % 16 == 0 else gather_plain
    lenv, renv, tensor = collect(
        nsec, nmpo, mpo, left_env, right_env, left_local, right_owner, right_local, blk_dev
    )
    moved = jnp.einsum("wkml,klpr->kmwpr", lenv, psi, preferred_element_type=F32).astype(BF16)
    mixed = jnp.einsum("wvqp,kmwpr->kmqvr", tensor, moved, preferred_element_type=F32).astype(BF16)
    result = jnp.einsum("kmqvr,vktr->kmqt", mixed, renv, preferred_element_type=F32).astype(BF16)
    return result.reshape(blk_dev, local_rows * phys * width)


def solution(mesh):
    placed = (
        P(("groups", "sector"), None, None, None),
        P("mpo", ("groups", "sector"), None, None),
        P(("groups", "mpo"), None, None, None),
        P("mpo", ("groups", "sector"), None, None),
        P("groups"),
        P("groups"),
        P("groups"),
    )
    return jax.shard_map(
        body, mesh=mesh, in_specs=placed, out_specs=P(("groups", "sector"), "mpo"), check_vma=False
    )
```

```python
import functools

import jax
import jax.numpy as jnp
from jax import lax
from jax.experimental import pallas as pl
from jax.experimental.pallas import tpu as pltpu
from jax.sharding import PartitionSpec as P

F32 = jnp.float32
BF16 = jnp.bfloat16
MESH = pl.DeviceIdType.MESH


def exchange(
    nsec,
    nmpo,
    left_local_hbm,
    right_owner_hbm,
    right_local_hbm,
    left_env_hbm,
    right_env_hbm,
    mpo,
    lenv,
    renv,
    tensor,
    left_local,
    right_owner,
    right_local,
    left_env,
    right_env,
    load_sem,
    to_sector,
    to_mpo,
    sector_send,
    sector_recv,
    left_send,
    left_recv,
    tensor_send,
    tensor_recv,
    own_send,
    own_recv,
    *from_sector,
):
    blk_dev, local_rows = lenv.shape[1], lenv.shape[2]
    piece = from_sector[0].shape[1]
    cuts = to_sector.shape[2] // piece
    chunks = blk_dev * cuts
    me = lax.axis_index("sector")
    z = lax.axis_index("mpo")
    barrier = pltpu.get_barrier_semaphore()
    for d in range(1, nsec):
        pl.semaphore_signal(barrier, inc=1, device_id={"sector": lax.rem(me + d, nsec)}, device_id_type=MESH)
    for d in range(1, nmpo):
        pl.semaphore_signal(barrier, inc=1, device_id={"mpo": lax.rem(z + d, nmpo)}, device_id_type=MESH)

    loads = [
        pltpu.make_async_copy(src, dst, load_sem.at[i])
        for i, (src, dst) in enumerate(
            (
                (right_local_hbm, right_local),
                (right_env_hbm.at[0], right_env),
                (left_local_hbm, left_local),
                (left_env_hbm.at[0], left_env),
                (right_owner_hbm, right_owner),
                (mpo.at[0], tensor.at[z]),
            )
        )
    ]
    for load in loads:
        load.start()
    loads[0].wait()
    loads[1].wait()
    pl.semaphore_wait(barrier, nsec + nmpo - 2)

    def span(c):
        return pl.ds(c % cuts * piece, piece)

    def sector_copy(c, d):
        peer = lax.rem(me + d, nsec)
        return pltpu.make_async_remote_copy(
            src_ref=to_sector.at[c // cuts, peer, span(c)],
            dst_ref=from_sector[c].at[me],
            send_sem=sector_send.at[c, d],
            recv_sem=sector_recv.at[c, d],
            device_id={"sector": peer},
            device_id_type=MESH,
        )

    def left_copy(d):
        peer = lax.rem(z + d, nmpo)
        return pltpu.make_async_remote_copy(
            src_ref=to_mpo.at[peer],
            dst_ref=lenv.at[z],
            send_sem=left_send.at[d],
            recv_sem=left_recv.at[d],
            device_id={"mpo": peer},
            device_id_type=MESH,
        )

    def tensor_copy(d):
        return pltpu.make_async_remote_copy(
            src_ref=tensor.at[z],
            dst_ref=tensor.at[z],
            send_sem=tensor_send.at[d],
            recv_sem=tensor_recv.at[d],
            device_id={"mpo": lax.rem(z + d, nmpo)},
            device_id_type=MESH,
        )

    def own_copy(c, d):
        return pltpu.make_async_remote_copy(
            src_ref=renv.at[z, c // cuts, span(c)],
            dst_ref=renv.at[z, c // cuts, span(c)],
            send_sem=own_send.at[d, c],
            recv_sem=own_recv.at[d, c],
            device_id={"mpo": lax.rem(z + d, nmpo)},
            device_id_type=MESH,
        )

    for k in range(blk_dev):
        for t in range(nsec):
            to_sector[k, t] = right_env[right_local[t * blk_dev + k]]
        for c in range(k * cuts, (k + 1) * cuts):
            for d in range(1, nsec):
                sector_copy(c, d).start()
    loads[2].wait()
    loads[3].wait()
    for k in range(blk_dev):
        picked = left_env[left_local[me * blk_dev + k]]
        for j in range(nmpo):
            to_mpo[j, k] = picked[j * local_rows : (j + 1) * local_rows]
    for d in range(1, nmpo):
        left_copy(d).start()
    lenv[z] = to_mpo[z]
    loads[5].wait()
    for d in range(1, nmpo):
        tensor_copy(d).start()
    loads[4].wait()

    for c in range(chunks):
        from_sector[c][me] = to_sector[c // cuts, me, span(c)]
        for d in range(1, nsec):
            sector_copy(c, d).wait_recv()
        renv[z, c // cuts, span(c)] = from_sector[c][right_owner[me * blk_dev + c // cuts]]

        for d in range(1, nmpo):
            own_copy(c, d).start()

    for d in range(1, nmpo):
        left_copy(d).wait()
        tensor_copy(d).wait()
    for c in range(chunks):
        for d in range(1, nmpo):
            own_copy(c, d).wait()
        for d in range(1, nsec):
            sector_copy(c, d).wait_send()


def gather(nsec, nmpo, mpo, left_env, right_env, left_local, right_owner, right_local, blk_dev):
    rows, width = right_env.shape[2:]
    local_rows = rows // nmpo
    cuts = 1
    chunks = blk_dev * cuts
    vmem = pl.BlockSpec(memory_space=pltpu.VMEM)
    hbm = pl.BlockSpec(memory_space=pltpu.HBM)
    dma = pltpu.SemaphoreType.DMA
    return pl.pallas_call(
        functools.partial(exchange, nsec, nmpo),
        out_shape=(
            jax.ShapeDtypeStruct((nmpo, blk_dev, local_rows, rows), BF16),
            jax.ShapeDtypeStruct((nmpo, blk_dev, rows, width), BF16),
            jax.ShapeDtypeStruct((nmpo,) + mpo.shape[1:], BF16),
        ),
        in_specs=[hbm] * 6,
        out_specs=(vmem,) * 3,
        scratch_shapes=[
            pltpu.SMEM(left_local.shape, left_local.dtype),
            pltpu.SMEM(right_owner.shape, right_owner.dtype),
            pltpu.SMEM(right_local.shape, right_local.dtype),
            pltpu.VMEM(left_env.shape[1:], BF16),
            pltpu.VMEM(right_env.shape[1:], BF16),
            dma((6,)),
            pltpu.VMEM((blk_dev, nsec, rows, width), BF16),
            pltpu.VMEM((nmpo, blk_dev, local_rows, rows), BF16),
            dma((chunks, nsec)),
            dma((chunks, nsec)),
            dma((nmpo,)),
            dma((nmpo,)),
            dma((nmpo,)),
            dma((nmpo,)),
            dma((nmpo, chunks)),
            dma((nmpo, chunks)),
        ]
        + [pltpu.VMEM((nsec, rows // cuts, width), BF16)] * chunks,
        compiler_params=pltpu.CompilerParams(
            collective_id=0, has_side_effects=True, vmem_limit_bytes=63 * 2**20
        ),
    )(left_local, right_owner, right_local, left_env, right_env, mpo)


def gather_plain(nsec, nmpo, mpo, left_env, right_env, left_local, right_owner, right_local, blk_dev):
    rows, width = right_env.shape[2:]
    local_rows = rows // nmpo
    me = lax.axis_index("sector")
    first = me * blk_dev
    slots = jnp.where(right_owner == me, right_local, 0)
    wanted = [lax.dynamic_index_in_dim(right_env[0], slots[i], 0) for i in range(nsec * blk_dev)]
    outgoing = jnp.concatenate(wanted).reshape(nsec, blk_dev, rows, width)
    arrived = lax.all_to_all(outgoing, "sector", split_axis=0, concat_axis=0, tiled=True)

    own_left, own_env = [], []
    for i in range(blk_dev):
        own_left.append(
            lax.dynamic_index_in_dim(left_env[0], left_local[first + i], 0).reshape(nmpo, local_rows, rows)
        )
        own_env.append(lax.dynamic_index_in_dim(arrived[:, i], right_owner[first + i], 0))
    env_rows = blk_dev * rows
    own_env = jnp.concatenate(own_env).reshape(1, env_rows, width)
    left_rows = blk_dev * local_rows
    own_mpo = mpo[0].reshape(1, -1, width)
    packed = jnp.concatenate(
        own_left
        + [
            jnp.broadcast_to(own_env, (nmpo, env_rows, width)),
            jnp.broadcast_to(own_mpo, (nmpo,) + own_mpo.shape[1:]),
        ],
        axis=1,
    )
    got = lax.all_to_all(packed, "mpo", split_axis=0, concat_axis=0, tiled=True)
    lenv = got[:, :left_rows].reshape(nmpo, blk_dev, local_rows, rows)
    renv = got[:, left_rows : left_rows + env_rows].reshape(nmpo, blk_dev, rows, width)
    tensor = got[:, left_rows + env_rows :].reshape((nmpo,) + mpo.shape[1:])

    return lenv, renv, tensor


def body(psi, left_env, mpo, right_env, left_local, right_owner, right_local):
    blk_dev, rows, phys, width = psi.shape
    nsec = lax.axis_size("sector")
    nmpo = lax.axis_size("mpo")
    local_rows = rows // nmpo
    collect = gather if local_rows % 16 == 0 else gather_plain
    lenv, renv, tensor = collect(
        nsec, nmpo, mpo, left_env, right_env, left_local, right_owner, right_local, blk_dev
    )
    moved = jnp.einsum("wkml,klpr->kmwpr", lenv, psi, preferred_element_type=F32).astype(BF16)
    mixed = jnp.einsum("wvqp,kmwpr->kmqvr", tensor, moved, preferred_element_type=F32).astype(BF16)
    result = jnp.einsum("kmqvr,vktr->kmqt", mixed, renv, preferred_element_type=F32).astype(BF16)
    return result.reshape(blk_dev, local_rows * phys * width)


def solution(mesh):
    placed = (
        P(("groups", "sector"), None, None, None),
        P("mpo", ("groups", "sector"), None, None),
        P(("groups", "mpo"), None, None, None),
        P("mpo", ("groups", "sector"), None, None),
        P("groups"),
        P("groups"),
        P("groups"),
    )
    return jax.shard_map(
        body, mesh=mesh, in_specs=placed, out_specs=P(("groups", "sector"), "mpo"), check_vma=False
    )
```
